32 devices in a mesh: sub: 8 (over y, x, core), col: 4 (over z).
Axes of the slice: x: 2, y: 2, z: 4, core: 2. Of those that a mesh axis runs over, the one named last changes fastest.
Arguments:
- perm: float32 [512, 512, 128], P('sub', 'col'), may hold values from 0.1 to 10
- accum: float32 [512, 512, 128], P('sub', 'col'), may hold values from 0.05 to 2
- rhs: float32 [512, 512, 128], P('sub', 'col'), may hold values from -24 to 24
- depth_x: int32 [16, 512], P('sub', 'col'), may hold values from 0 to 4, as said below
- depth_y: int32 [512, 8], P('sub', 'col'), may hold values from 0 to 4, as said below
Outputs:
- pressure: float32 [512, 512, 128], P('sub', 'col')
The draws below stay inside these ranges and needn't reach their ends.
Inputs may be any that keep to these rules, and one draw needn't show every extreme that they name: Both sides of one interface share its depth: depth_x[2 s + 1, j] = depth_x[2 s + 2, j] and depth_y[i, 2 c + 1] = depth_y[i, 2 c + 2]; faces on the grid's boundary have depth 0; the depth 4 occurs. `depth_y`: as for depth_x, along the second dimension.
All inputs are finite; a program needn't handle non-finite values.
Results may differ from the reference program's by a relative error of at most 0.0003.
Values sent between devices are 32-bit elements; how exact they have to be, the bound alone decides.
A program may use at most 192 MiB of HBM per device.

```python
import math
import jax
import jax.numpy as jnp
from jax import lax

SX = 64
SY = 128
NZ = 128
OVL = 4
SWEEPS = 3
ITERS = 2
NX = 512
NY = 512
N_SUB = 8
N_COL = 4


def draw_depth_x(key, part):
    interior_depth = jax.random.randint(jax.random.fold_in(key, 11), (N_SUB - 1, NY), 0, OVL + 1, dtype=jnp.int32)
    interior_depth = interior_depth.at[0, 0].set(OVL)
    boundary = jnp.zeros((1, NY), jnp.int32)
    interfaces = jnp.concatenate([boundary, interior_depth, boundary], axis=0)
    return jnp.stack([interfaces[:-1], interfaces[1:]], axis=1).reshape(2 * N_SUB, NY)


def draw_depth_y(key, part):
    interior_depth = jax.random.randint(jax.random.fold_in(key, 12), (NX, N_COL - 1), 0, OVL + 1, dtype=jnp.int32)
    interior_depth = interior_depth.at[0, 0].set(OVL)
    boundary = jnp.zeros((NX, 1), jnp.int32)
    interfaces = jnp.concatenate([boundary, interior_depth, boundary], axis=1)
    return jnp.stack([interfaces[:, :-1], interfaces[:, 1:]], axis=2).reshape(NX, 2 * N_COL)


def block_scale(key, dims, shards, least, high):
    gain = 1.0
    for dim, parts in shards:
        draws = jax.random.uniform(jax.random.fold_in(jax.random.fold_in(key, 6), dim), (parts,), jnp.float32, least / len(shards), high / len(shards))
        gain = gain * jnp.repeat(jnp.exp(draws), dims[dim] // parts).reshape((-1,) + (1,) * (len(dims) - 1 - dim))
    return gain


def normal_values(stream_key, extent, deviation, limit, shards=(), held_as=jnp.bfloat16):
    result = jax.random.normal(stream_key, extent, jnp.float32) * deviation
    if len(shards) > 0:
        result = block_scale(stream_key, extent, shards, -0.22, 0.18) * result
    return jnp.clip(result, min=-limit, max=limit).astype(held_as)


def setup_inputs(seed: int = 0) -> dict:
    key_list = jax.random.split(jax.random.key(seed), 6)
    perm = jnp.clip(jnp.exp(math.log(10.0) - 4.6051702 * jax.random.uniform(key_list[0], (NX, NY, NZ), jnp.float32) ** block_scale(key_list[0], (NX, NY, NZ), ((0, 8), (1, 4)), -0.2, 0.2)), 0.1, 10.0)
    accum = jnp.clip(jnp.exp(math.log(2.0) - 3.6888794 * jax.random.uniform(key_list[1], (NX, NY, NZ), jnp.float32) ** block_scale(key_list[1], (NX, NY, NZ), ((0, 8), (1, 4)), -0.2, 0.2)), 0.05, 2.0)
    rhs = normal_values(key_list[2], (NX, NY, NZ), 4.0, 24.0, ((0, 8), (1, 4)), jnp.float32)
    depth_x = draw_depth_x(jax.random.fold_in(key_list[5], 71), 0)
    depth_y = draw_depth_y(jax.random.fold_in(key_list[5], 71), 0)
    return {"perm": perm, "accum": accum, "rhs": rhs, "depth_x": depth_x, "depth_y": depth_y}


VERTICAL = 0.1


def harmonic(first_perm, second_perm):
    return 2.0 * first_perm * second_perm / (first_perm + second_perm)


def coefficients(perm_padded, accum_centre, inside_x, inside_y):
    inside = inside_x[:, None, None] & inside_y[None, :, None]
    perm_safe = jnp.where(inside, perm_padded, 1.0)
    across_x = harmonic(perm_safe[:-1, 1:-1], perm_safe[1:, 1:-1])
    open_x = (inside_x[:-1] & inside_x[1:])[:, None, None]
    across_x = jnp.where(open_x, across_x, 0.0)
    across_y = harmonic(perm_safe[1:-1, :-1], perm_safe[1:-1, 1:])
    open_y = (inside_y[:-1] & inside_y[1:])[None, :, None]
    across_y = jnp.where(open_y, across_y, 0.0)
    centre = perm_safe[1:-1, 1:-1]
    upward = VERTICAL * harmonic(centre[:, :, :-1], centre[:, :, 1:])
    bottom = jnp.zeros_like(centre[:, :, :1])
    lower_z = jnp.concatenate([bottom, upward], axis=2)
    upper_z = jnp.concatenate([upward, bottom], axis=2)
    lower_x = across_x[:-1]
    upper_x = across_x[1:]
    lower_y = across_y[:, :-1]
    upper_y = across_y[:, 1:]
    diagonal = accum_centre + lower_x + upper_x + lower_y + upper_y + lower_z + upper_z
    return (diagonal, lower_x, upper_x, lower_y, upper_y, lower_z, upper_z)


def neighbour_sum(padded, coeffs):
    diagonal, lower_x, upper_x, lower_y, upper_y, lower_z, upper_z = coeffs
    centre = padded[1:-1, 1:-1]
    bottom = jnp.zeros_like(centre[:, :, :1])
    below = jnp.concatenate([bottom, centre[:, :, :-1]], axis=2)
    above = jnp.concatenate([centre[:, :, 1:], bottom], axis=2)
    total = lower_x * padded[:-2, 1:-1] + upper_x * padded[2:, 1:-1]
    total = total + lower_y * padded[1:-1, :-2] + upper_y * padded[1:-1, 2:]
    return total + lower_z * below + upper_z * above


def operate(padded, coeffs):
    return coeffs[0] * padded[1:-1, 1:-1] - neighbour_sum(padded, coeffs)


def membership(depth_lo_hi_x, depth_lo_hi_y, inside_x, inside_y, block_x, block_y, margin):
    row_ids = jnp.arange(block_x + 2 * margin, dtype=jnp.int32)[:, None]
    column_ids = jnp.arange(block_y + 2 * margin, dtype=jnp.int32)[None, :]
    in_rows = (row_ids >= margin) & (row_ids < margin + block_x)
    in_columns = (column_ids >= margin) & (column_ids < margin + block_y)
    low_x = jnp.pad(depth_lo_hi_x[0], (margin, margin))[None, :]
    high_x = jnp.pad(depth_lo_hi_x[1], (margin, margin))[None, :]
    low_y = jnp.pad(depth_lo_hi_y[:, 0], (margin, margin))[:, None]
    high_y = jnp.pad(depth_lo_hi_y[:, 1], (margin, margin))[:, None]
    member = in_rows & in_columns
    member = member | ((row_ids < margin) & in_columns & ((margin - 1 - row_ids) < low_x))
    member = member | ((row_ids >= margin + block_x) & in_columns & ((row_ids - margin - block_x) < high_x))
    member = member | ((column_ids < margin) & in_rows & ((margin - 1 - column_ids) < low_y))
    member = member | ((column_ids >= margin + block_y) & in_rows & ((column_ids - margin - block_y) < high_y))
    return member & inside_x[:, None] & inside_y[None, :]


def local_solve(resid_ext, coeffs, diag_safe, member_cells):
    correction = jnp.zeros_like(resid_ext)
    for sweep_index in range(SWEEPS):
        padded = jnp.pad(correction, ((1, 1), (1, 1), (0, 0)))
        correction = jnp.where(member_cells, (resid_ext + neighbour_sum(padded, coeffs)) / diag_safe, 0.0)
    return correction


def reference(perm, accum, rhs, depth_x, depth_y):
    total_x = SX * N_SUB
    total_y = SY * N_COL
    margin = OVL
    grid_x = jnp.arange(total_x + 2, dtype=jnp.int32) - 1
    grid_y = jnp.arange(total_y + 2, dtype=jnp.int32) - 1
    global_coeffs = coefficients(jnp.pad(perm, ((1, 1), (1, 1), (0, 0))), accum,
                                 (grid_x >= 0) & (grid_x < total_x), (grid_y >= 0) & (grid_y < total_y))
    perm_wide = jnp.pad(perm, ((margin + 1, margin + 1), (margin + 1, margin + 1), (0, 0)))
    accum_wide = jnp.pad(accum, ((margin, margin), (margin, margin), (0, 0)))
    ext_x = SX + 2 * margin
    ext_y = SY + 2 * margin
    pressure = jnp.zeros_like(rhs)
    for iteration in range(ITERS):
        if iteration == 0:
            residual = rhs
        else:
            residual = rhs - operate(jnp.pad(pressure, ((1, 1), (1, 1), (0, 0))), global_coeffs)
        resid_wide = jnp.pad(residual, ((margin, margin), (margin, margin), (0, 0)))

        def visit(totals, domain):
            sub_index = domain // N_COL
            col_index = domain % N_COL
            start_x = sub_index * SX
            start_y = col_index * SY
            zero_index = jnp.zeros((), jnp.int32)
            perm_block = lax.dynamic_slice(perm_wide, (start_x, start_y, zero_index), (ext_x + 2, ext_y + 2, NZ))
            accum_block = lax.dynamic_slice(accum_wide, (start_x, start_y, zero_index), (ext_x, ext_y, NZ))
            resid_block = lax.dynamic_slice(resid_wide, (start_x, start_y, zero_index), (ext_x, ext_y, NZ))
            row_global = start_x - (margin + 1) + jnp.arange(ext_x + 2, dtype=jnp.int32)
            column_global = start_y - (margin + 1) + jnp.arange(ext_y + 2, dtype=jnp.int32)
            inside_x = (row_global >= 0) & (row_global < total_x)
            inside_y = (column_global >= 0) & (column_global < total_y)
            coeffs = coefficients(perm_block, accum_block, inside_x, inside_y)
            block_depth_x = lax.dynamic_slice(depth_x, (2 * sub_index, start_y), (2, SY))
            block_depth_y = lax.dynamic_slice(depth_y, (start_x, 2 * col_index), (SX, 2))
            member = membership(block_depth_x, block_depth_y, inside_x[1:-1], inside_y[1:-1], SX, SY, margin)
            member_cells = member[:, :, None]
            diag_safe = jnp.where(member_cells, coeffs[0], 1.0)
            correction = local_solve(resid_block, coeffs, diag_safe, member_cells)
            summed, covered = totals
            previous = lax.dynamic_slice(summed, (start_x, start_y, zero_index), (ext_x, ext_y, NZ))
            summed = lax.dynamic_update_slice(summed, previous + correction, (start_x, start_y, zero_index))
            seen = lax.dynamic_slice(covered, (start_x, start_y), (ext_x, ext_y))
            covered = lax.dynamic_update_slice(covered, seen + member.astype(jnp.float32), (start_x, start_y))
            return (summed, covered), None

        initial = (jnp.zeros((total_x + 2 * margin, total_y + 2 * margin, NZ), jnp.float32),
                   jnp.zeros((total_x + 2 * margin, total_y + 2 * margin), jnp.float32))
        totals, ignored = lax.scan(visit, initial, jnp.arange(N_SUB * N_COL, dtype=jnp.int32))
        summed, covered = totals
        owned_sum = summed[margin:margin + total_x, margin:margin + total_y]
        owned_cover = covered[margin:margin + total_x, margin:margin + total_y]
        pressure = pressure + owned_sum / owned_cover[:, :, None]
    return pressure
```

```python
import functools

import jax
import jax.numpy as jnp
from jax import lax
from jax.experimental import pallas as pl
from jax.experimental.pallas import tpu as pltpu
from jax.sharding import PartitionSpec as P

OVL = 4
VERTICAL = 0.1
MESH = pl.DeviceIdType.MESH

PADX = 5
PADY = 8
DIRS = ((-1, 0), (1, 0), (0, -1), (0, 1), (-1, -1), (-1, 1), (1, -1), (1, 1))


def recip(value):
    guess = pl.reciprocal(value, approx=True)
    return guess * (2.0 - value * guess)


def harmonic(first, second):
    return 2.0 * first * second * recip(first + second)


def kernel(n_sub, n_col, bx, by, perm, accum, rhs, dx_ref, dy_ref, out,
           pm, w, r, b, c, fx, fy, fz, pr, sx, sy, ssem, rsem, lsem):
    nz = 128
    s = lax.axis_index("sub")
    k = lax.axis_index("col")
    ex, ey = bx + 2 * PADX, by + 2 * PADY
    nbx, nby = (bx + 8) // 8, (by + 8) // 8
    x_end, y_end = PADX + bx, PADY + by

    def exists(d):
        ok = None
        for coord, step, count in ((s, d[0], n_sub), (k, d[1], n_col)):
            if step == -1:
                test = coord > 0
            elif step == 1:
                test = coord < count - 1
            else:
                continue
            ok = test if ok is None else ok & test
        return ok

    def device(d):
        return (s + d[0], k + d[1])

    own_x, own_y = pl.ds(PADX, bx), pl.ds(PADY, by)
    local = [
        pltpu.make_async_copy(src, dst.at[own_x, own_y, :], lsem.at[i])
        for i, (src, dst) in enumerate(((perm, pm), (accum, w), (rhs, r)))
    ]
    for copy in local:
        copy.start()

    def fill(ref, value):
        ref[0:PADX, :, :] = jnp.full((PADX, ey, nz), value, jnp.float32)
        ref[x_end:ex, :, :] = jnp.full((PADX, ey, nz), value, jnp.float32)
        ref[PADX:x_end, 0:PADY, :] = jnp.full((bx, PADY, nz), value, jnp.float32)
        ref[PADX:x_end, y_end:ey, :] = jnp.full((bx, PADY, nz), value, jnp.float32)

    fill(pm, 1.0)
    fill(w, 1.0)
    fill(r, 0.0)
    fill(b, 0.0)
    fill(c, 0.0)
    fill(pr, 0.0)
    sx[...] = jnp.zeros(sx.shape, jnp.float32)
    sy[...] = jnp.zeros(sy.shape, jnp.float32)

    barrier = pltpu.get_barrier_semaphore()
    arrivals = jnp.int32(0)
    for d in DIRS:
        @pl.when(exists(d))
        def _(d=d):
            pl.semaphore_signal(barrier, inc=1, device_id=device(d), device_id_type=MESH)
        arrivals = arrivals + jnp.where(exists(d), 1, 0).astype(jnp.int32)
    pl.semaphore_wait(barrier, arrivals)

    counter = [0]

    def remote(src, dst, d):
        i = counter[0]
        counter[0] += 1
        return d, pltpu.make_async_remote_copy(
            src_ref=src, dst_ref=dst, send_sem=ssem.at[i], recv_sem=rsem.at[i],
            device_id=device(d), device_id_type=MESH)

    def start(copies):
        for d, copy in copies:
            pl.when(exists(d))(copy.start)

    def wait_recv(copies):
        for d, copy in copies:
            pl.when(exists((-d[0], -d[1])))(copy.wait_recv)

    def wait_send(copies):
        for d, copy in copies:
            pl.when(exists(d))(copy.wait_send)

    def halo(src, ox, oy, dst, d, width):
        def span(step, offset, extent, pad, thick):
            if step == 0:
                return pl.ds(offset, extent), pl.ds(pad, extent)
            if step == 1:
                return pl.ds(offset + extent - thick, thick), pl.ds(pad - thick, thick)
            return pl.ds(offset, thick), pl.ds(pad + extent, thick)

        sxs, dxs = span(d[0], ox, bx, PADX, width)
        sys_, dys = span(d[1], oy, by, PADY, YW(width))
        return remote(src.at[sxs, sys_, :], dst.at[dxs, dys, :], d)

    def YW(width):
        return 8

    halos = [halo(perm, 0, 0, pm, d, 5) for d in DIRS]
    halos += [halo(accum, 0, 0, w, d, 4) for d in DIRS[:4]]
    halos += [halo(rhs, 0, 0, r, d, 4) for d in DIRS[:4]]
    start(halos)

    def at(ref, x0, y0, rows=8, columns=8):
        return ref[pl.ds(x0, rows), pl.ds(y0, columns), :]

    def stencil(ref, x0, y0):
        wide = at(ref, x0 - 1, y0, 10)
        centre = wide[1:9]
        face = at(fx, x0 - 1, y0, 9)
        total = face[0:8] * wide[0:8] + face[1:9] * wide[2:10]
        total = total + at(fy, x0, y0) * at(ref, x0, y0 - 1)
        total = total + at(fy, x0, y0 + 1) * at(ref, x0, y0 + 1)
        up = at(fz, x0, y0)
        total = total + up * pltpu.roll(centre, nz - 1, 2)
        total = total + pltpu.roll(up * centre, 1, 2)
        return total, centre

    def coefficients(x0, y0, frame):
        wide = at(pm, x0 - 1, y0, 10)
        centre = wide[1:9]
        across_x = harmonic(wide[0:9], wide[1:10])
        across_y0 = harmonic(at(pm, x0, y0 - 1), centre)
        across_y1 = harmonic(centre, at(pm, x0, y0 + 1))
        lane = lax.broadcasted_iota(jnp.int32, (8, 8, nz), 2)
        up = VERTICAL * harmonic(centre, pltpu.roll(centre, nz - 1, 2))
        up = jnp.where(lane < nz - 1, up, 0.0)
        if frame:
            row = x0 - 1 + lax.broadcasted_iota(jnp.int32, (9, 8, nz), 0)
            shut = (row == jnp.where(s == 0, PADX - 1, -1)) | (
                row == jnp.where(s == n_sub - 1, x_end - 1, -1))
            across_x = jnp.where(shut, 0.0, across_x)
            column = y0 + lax.broadcasted_iota(jnp.int32, (8, 8, nz), 1)
            first = jnp.where(k == 0, PADY, -1)
            last = jnp.where(k == n_col - 1, y_end, -1)
            across_y0 = jnp.where((column == first) | (column == last), 0.0, across_y0)
            across_y1 = jnp.where((column + 1 == first) | (column + 1 == last), 0.0, across_y1)
        diagonal = (at(w, x0, y0) + across_x[0:8] + across_x[1:9] + across_y0 + across_y1
                    + up + pltpu.roll(up, 1, 2))
        inverse = recip(diagonal)
        if frame:
            row = row[0:8] + 1
            low_x, high_x = dx_ref[0, pl.ds(y0, 8), :], dx_ref[1, pl.ds(y0, 8), :]
            low_y, high_y = dy_ref[0, pl.ds(x0, 8), :, :], dy_ref[1, pl.ds(x0, 8), :, :]
            member = (row >= PADX) & (row < x_end) & (column >= PADY) & (column < y_end)
            member = member | ((row < PADX) & (PADX - 1 - row < low_x[None]))
            member = member | ((row >= x_end) & (row - x_end < high_x[None]))
            member = member | ((column < PADY) & (PADY - 1 - column < low_y))
            member = member | ((column >= y_end) & (column - y_end < high_y))
            inverse = jnp.where(member, inverse, 0.0)
        fx[pl.ds(x0 - 1, 9), pl.ds(y0, 8), :] = across_x
        fy[pl.ds(x0, 8), pl.ds(y0, 8), :] = across_y0
        fy[pl.ds(x0, 8), pl.ds(y0 + 1, 8), :] = across_y1
        fz[pl.ds(x0, 8), pl.ds(y0, 8), :] = up
        w[pl.ds(x0, 8), pl.ds(y0, 8), :] = inverse
        b[pl.ds(x0, 8), pl.ds(y0, 8), :] = inverse * at(r, x0, y0)

    def second_sweep(x0, y0):
        total, _ = stencil(b, x0, y0)
        c[pl.ds(x0, 8), pl.ds(y0, 8), :] = at(b, x0, y0) + at(w, x0, y0) * total

    def third_sweep(x0, y0):
        total, _ = stencil(c, x0, y0)
        return at(b, x0, y0) + at(w, x0, y0) * total

    def third_frame(x0, y0):
        b[pl.ds(x0, 8), pl.ds(y0, 8), :] = third_sweep(x0, y0)

    def third_first(x0, y0):
        pr[pl.ds(x0, 8), pl.ds(y0, 8), :] = third_sweep(x0, y0)

    def third_last(x0, y0):
        pr[pl.ds(x0, 8), pl.ds(y0, 8), :] = at(pr, x0, y0) + third_sweep(x0, y0)

    def restart(x0, y0):
        total, centre = stencil(pr, x0, y0)
        weight = at(w, x0, y0)
        b[pl.ds(x0, 8), pl.ds(y0, 8), :] = jnp.where(
            weight > 0.0, weight * (at(r, x0, y0) + total) - centre, 0.0)

    def interior(body):
        def outer(j, carry):
            def inner(i, carry):
                body(1 + 8 * i, 4 + 8 * j)
                return carry
            return lax.fori_loop(1, nbx - 1, inner, carry)
        lax.fori_loop(1, nby - 1, outer, 0)

    def frame(body):
        def along_y(j, carry):
            body(1, 4 + 8 * j)
            body(1 + 8 * (nbx - 1), 4 + 8 * j)
            return carry
        lax.fori_loop(0, nby, along_y, 0)

        def along_x(i, carry):
            body(1 + 8 * i, 4)
            body(1 + 8 * i, 4 + 8 * (nby - 1))
            return carry
        lax.fori_loop(1, nbx - 1, along_x, 0)

    def gather(turn, x0, y0, side_x, side_y):
        own = at(b, x0, y0, 4)
        before = at(pr, x0, y0, 4)
        row = x0 + lax.broadcasted_iota(jnp.int32, (4, 8, nz), 0)
        column = y0 + lax.broadcasted_iota(jnp.int32, (4, 8, nz), 1)
        total = own
        if side_x is not None:
            total = total + sx[turn, side_x, :, pl.ds(y0 - PADY, 8), :]
        if side_y is not None:
            total = total + sy[turn, side_y, pl.ds(x0 - PADX, 4), :, :]
        cover = 1.0 + (row - PADX < dx_ref[0, pl.ds(y0, 8), :][None]).astype(jnp.float32)
        cover = cover + (x_end - 1 - row < dx_ref[1, pl.ds(y0, 8), :][None]).astype(jnp.float32)
        cover = cover + (column - PADY < dy_ref[0, pl.ds(x0, 4), :, :]).astype(jnp.float32)
        cover = cover + (y_end - 1 - column < dy_ref[1, pl.ds(x0, 4), :, :]).astype(jnp.float32)
        total = total / cover
        if turn == 1:
            total = before + total
        if side_x is None:
            edge = (column < PADY + 4) if side_y == 0 else (column >= y_end - 4)
            total = jnp.where(edge, total, before)
        pr[pl.ds(x0, 4), pl.ds(y0, 8), :] = total

    def gather_all(turn):
        top = x_end - 4
        for side_y, y0 in ((0, PADY), (1, y_end - 8)):
            gather(turn, PADX, y0, 0, side_y)
            gather(turn, top, y0, 1, side_y)

            def along_x(i, carry, y0=y0, side_y=side_y):
                gather(turn, PADX + 4 * i, y0, None, side_y)
                return carry
            lax.fori_loop(1, bx // 4 - 1, along_x, 0)

        def along_y(j, carry):
            gather(turn, PADX, PADY + 8 * j, 0, None)
            gather(turn, top, PADY + 8 * j, 1, None)
            return carry
        lax.fori_loop(1, by // 8 - 1, along_y, 0)

    def returns(turn):
        return [
            remote(b.at[pl.ds(PADX - 4, 4), own_y, :], sx.at[turn, 1], (-1, 0)),
            remote(b.at[pl.ds(x_end, 4), own_y, :], sx.at[turn, 0], (1, 0)),
            remote(b.at[own_x, pl.ds(0, 8), :], sy.at[turn, 1], (0, -1)),
            remote(b.at[own_x, pl.ds(y_end, 8), :], sy.at[turn, 0], (0, 1)),
        ]

    for copy in local:
        copy.wait()
    interior(functools.partial(coefficients, frame=False))
    wait_recv(halos)
    frame(functools.partial(coefficients, frame=True))
    interior(second_sweep)
    frame(second_sweep)
    frame(third_frame)
    back = returns(0)
    start(back)
    interior(third_first)
    wait_recv(back)
    gather_all(0)
    spread = [halo(pr, PADX, PADY, pr, d, 5) for d in DIRS]
    start(spread)
    wait_send(back)
    interior(restart)
    wait_recv(spread)
    frame(restart)
    interior(second_sweep)
    frame(second_sweep)
    frame(third_frame)
    back = returns(1)
    start(back)
    wait_send(spread)
    interior(third_last)
    wait_recv(back)
    gather_all(1)
    final = pltpu.make_async_copy(pr.at[own_x, own_y, :], out, lsem.at[0])
    final.start()
    wait_send(halos)
    wait_send(back)
    final.wait()


def shards(n_sub, n_col, perm, accum, rhs, depth_x, depth_y):
    bx, by, nz = perm.shape
    ex, ey = bx + 2 * PADX, by + 2 * PADY
    dx = jnp.broadcast_to(jnp.pad(depth_x, ((0, 0), (PADY, PADY)))[:, :, None], (2, ey, nz))
    dy = jnp.broadcast_to(
        jnp.pad(depth_y, ((PADX, PADX), (0, 0))).T[:, :, None, None], (2, ex, 8, nz))
    field = pltpu.VMEM((ex, ey, nz), jnp.float32)
    hbm = pl.BlockSpec(memory_space=pl.ANY)
    vmem = pl.BlockSpec(memory_space=pltpu.VMEM)
    copies = 16 + 4 + 8 + 4
    return pl.pallas_call(
        functools.partial(kernel, n_sub, n_col, bx, by),
        out_shape=jax.ShapeDtypeStruct((bx, by, nz), jnp.float32),
        in_specs=[hbm, hbm, hbm, vmem, vmem],
        out_specs=hbm,
        scratch_shapes=[field] * 9 + [
            pltpu.VMEM((2, 2, 4, by, nz), jnp.float32),
            pltpu.VMEM((2, 2, bx, 8, nz), jnp.float32),
            pltpu.SemaphoreType.DMA((copies,)),
            pltpu.SemaphoreType.DMA((copies,)),
            pltpu.SemaphoreType.DMA((3,)),
        ],
        compiler_params=pltpu.CompilerParams(
            collective_id=0, has_side_effects=True, vmem_limit_bytes=60 * 1024 * 1024),
        cost_estimate=pl.CostEstimate(
            flops=120 * bx * by * nz, bytes_accessed=16 * bx * by * nz, transcendentals=0),
    )(perm, accum, rhs, dx, dy)


def solution(mesh):
    placed = (
        P("sub", "col", None),
        P("sub", "col", None),
        P("sub", "col", None),
        P("sub", "col"),
        P("sub", "col"),
    )
    return jax.shard_map(
        functools.partial(shards, mesh.shape["sub"], mesh.shape["col"]),
        mesh=mesh, in_specs=placed, out_specs=P("sub", "col", None), check_vma=False
    )
```

```python
import functools

import jax
import jax.numpy as jnp
from jax import lax
from jax.experimental import pallas as pl
from jax.experimental.pallas import tpu as pltpu
from jax.sharding import PartitionSpec as P

OVL = 4
VERTICAL = 0.1
MESH = pl.DeviceIdType.MESH

PADX = 5
PADY = 8
DIRS = ((-1, 0), (1, 0), (0, -1), (0, 1), (-1, -1), (-1, 1), (1, -1), (1, 1))


def recip(value):
    guess = pl.reciprocal(value, approx=True)
    return guess * (2.0 - value * guess)


def harmonic(first, second):
    return 2.0 * first * second * recip(first + second)


def kernel(n_sub, n_col, bx, by, perm, accum, rhs, depth_x, depth_y, out,
           dx_ref, dy_ref, lane_y, pm, w, r, b, c, fx, fy, fz, pr, sx, sy, ssem, rsem, lsem):
    nz = 128
    s = lax.axis_index("sub")
    k = lax.axis_index("col")
    ex, ey = bx + 2 * PADX, by + 2 * PADY
    nbx, nby = (bx + 8) // 8, (by + 8) // 8
    x_end, y_end = PADX + bx, PADY + by

    def exists(d):
        ok = None
        for coord, step, count in ((s, d[0], n_sub), (k, d[1], n_col)):
            if step == -1:
                test = coord > 0
            elif step == 1:
                test = coord < count - 1
            else:
                continue
            ok = test if ok is None else ok & test
        return ok

    def device(d):
        return (s + d[0], k + d[1])

    own_x, own_y = pl.ds(PADX, bx), pl.ds(PADY, by)
    local = [
        pltpu.make_async_copy(src, dst.at[own_x, own_y, :], lsem.at[i])
        for i, (src, dst) in enumerate(((perm, pm), (accum, w), (rhs, r)))
    ]
    for copy in local:
        copy.start()

    def fill(ref, value):
        ref[0:PADX, :, :] = jnp.full((PADX, ey, nz), value, jnp.float32)
        ref[x_end:ex, :, :] = jnp.full((PADX, ey, nz), value, jnp.float32)
        ref[PADX:x_end, 0:PADY, :] = jnp.full((bx, PADY, nz), value, jnp.float32)
        ref[PADX:x_end, y_end:ey, :] = jnp.full((bx, PADY, nz), value, jnp.float32)

    fill(pm, 1.0)
    fill(w, 1.0)
    fill(r, 0.0)
    fill(b, 0.0)
    fill(c, 0.0)
    fill(pr, 0.0)
    sx[...] = jnp.zeros(sx.shape, jnp.float32)
    sy[...] = jnp.zeros(sy.shape, jnp.float32)

    dx_ref[...] = jnp.zeros(dx_ref.shape, jnp.int32)
    dy_ref[...] = jnp.zeros(dy_ref.shape, jnp.int32)
    for side in range(2):
        dx_ref[side, own_y, :] = jnp.broadcast_to(depth_x[side:side + 1, :], (nz, by)).T
        lane_y[side] = jnp.broadcast_to(depth_y[:, side:side + 1], (bx, nz))

    def spread_depth(i, carry):
        for side in range(2):
            dy_ref[side, PADX + i] = jnp.broadcast_to(lane_y[side, pl.ds(i, 1), :], (8, nz))
        return carry

    barrier = pltpu.get_barrier_semaphore()
    arrivals = jnp.int32(0)
    for d in DIRS:
        @pl.when(exists(d))
        def _(d=d):
            pl.semaphore_signal(barrier, inc=1, device_id=device(d), device_id_type=MESH)
        arrivals = arrivals + jnp.where(exists(d), 1, 0).astype(jnp.int32)
    pl.semaphore_wait(barrier, arrivals)

    counter = [0]

    def remote(src, dst, d):
        i = counter[0]
        counter[0] += 1
        return d, pltpu.make_async_remote_copy(
            src_ref=src, dst_ref=dst, send_sem=ssem.at[i], recv_sem=rsem.at[i],
            device_id=device(d), device_id_type=MESH)

    def start(copies):
        for d, copy in copies:
            pl.when(exists(d))(copy.start)

    def wait_recv(copies):
        for d, copy in copies:
            pl.when(exists((-d[0], -d[1])))(copy.wait_recv)

    def wait_send(copies):
        for d, copy in copies:
            pl.when(exists(d))(copy.wait_send)

    def halo(src, ox, oy, dst, d, width):
        def span(step, offset, extent, pad, thick):
            if step == 0:
                return pl.ds(offset, extent), pl.ds(pad, extent)
            if step == 1:
                return pl.ds(offset + extent - thick, thick), pl.ds(pad - thick, thick)
            return pl.ds(offset, thick), pl.ds(pad + extent, thick)

        sxs, dxs = span(d[0], ox, bx, PADX, width)
        sys_, dys = span(d[1], oy, by, PADY, width)
        return remote(src.at[sxs, sys_, :], dst.at[dxs, dys, :], d)

    halos = [halo(perm, 0, 0, pm, d, 5) for d in DIRS]
    halos += [halo(accum, 0, 0, w, d, 4) for d in DIRS[:4]]
    halos += [halo(rhs, 0, 0, r, d, 4) for d in DIRS[:4]]
    start(halos)
    lax.fori_loop(0, bx, spread_depth, 0, unroll=8)

    def at(ref, x0, y0, rows=8, columns=8):
        return ref[pl.ds(x0, rows), pl.ds(y0, columns), :]

    def stencil(ref, x0, y0):
        wide = at(ref, x0 - 1, y0, 10)
        centre = wide[1:9]
        face = at(fx, x0 - 1, y0, 9)
        total = face[0:8] * wide[0:8] + face[1:9] * wide[2:10]
        total = total + at(fy, x0, y0) * at(ref, x0, y0 - 1)
        total = total + at(fy, x0, y0 + 1) * at(ref, x0, y0 + 1)
        up = at(fz, x0, y0)
        total = total + up * pltpu.roll(centre, nz - 1, 2)
        total = total + pltpu.roll(up * centre, 1, 2)
        return total, centre

    def coefficients(x0, y0, frame):
        wide = at(pm, x0 - 1, y0, 10)
        centre = wide[1:9]
        across_x = harmonic(wide[0:9], wide[1:10])
        across_y0 = harmonic(at(pm, x0, y0 - 1), centre)
        across_y1 = harmonic(centre, at(pm, x0, y0 + 1))
        lane = lax.broadcasted_iota(jnp.int32, (8, 8, nz), 2)
        up = VERTICAL * harmonic(centre, pltpu.roll(centre, nz - 1, 2))
        up = jnp.where(lane < nz - 1, up, 0.0)
        if frame:
            row = x0 - 1 + lax.broadcasted_iota(jnp.int32, (9, 8, nz), 0)
            shut = (row == jnp.where(s == 0, PADX - 1, -1)) | (
                row == jnp.where(s == n_sub - 1, x_end - 1, -1))
            across_x = jnp.where(shut, 0.0, across_x)
            column = y0 + lax.broadcasted_iota(jnp.int32, (8, 8, nz), 1)
            first = jnp.where(k == 0, PADY, -1)
            last = jnp.where(k == n_col - 1, y_end, -1)
            across_y0 = jnp.where((column == first) | (column == last), 0.0, across_y0)
            across_y1 = jnp.where((column + 1 == first) | (column + 1 == last), 0.0, across_y1)
        diagonal = (at(w, x0, y0) + across_x[0:8] + across_x[1:9] + across_y0 + across_y1
                    + up + pltpu.roll(up, 1, 2))
        inverse = recip(diagonal)
        if frame:
            row = row[0:8] + 1
            low_x, high_x = dx_ref[0, pl.ds(y0, 8), :], dx_ref[1, pl.ds(y0, 8), :]
            low_y, high_y = dy_ref[0, pl.ds(x0, 8), :, :], dy_ref[1, pl.ds(x0, 8), :, :]
            member = (row >= PADX) & (row < x_end) & (column >= PADY) & (column < y_end)
            member = member | ((row < PADX) & (PADX - 1 - row < low_x[None]))
            member = member | ((row >= x_end) & (row - x_end < high_x[None]))
            member = member | ((column < PADY) & (PADY - 1 - column < low_y))
            member = member | ((column >= y_end) & (column - y_end < high_y))
            inverse = jnp.where(member, inverse, 0.0)
        fx[pl.ds(x0 - 1, 9), pl.ds(y0, 8), :] = across_x
        fy[pl.ds(x0, 8), pl.ds(y0, 8), :] = across_y0
        fy[pl.ds(x0, 8), pl.ds(y0 + 1, 8), :] = across_y1
        fz[pl.ds(x0, 8), pl.ds(y0, 8), :] = up
        w[pl.ds(x0, 8), pl.ds(y0, 8), :] = inverse
        b[pl.ds(x0, 8), pl.ds(y0, 8), :] = inverse * at(r, x0, y0)

    def second_sweep(x0, y0):
        total, _ = stencil(b, x0, y0)
        c[pl.ds(x0, 8), pl.ds(y0, 8), :] = at(b, x0, y0) + at(w, x0, y0) * total

    def third_sweep(x0, y0):
        total, _ = stencil(c, x0, y0)
        return at(b, x0, y0) + at(w, x0, y0) * total

    def third_frame(x0, y0):
        b[pl.ds(x0, 8), pl.ds(y0, 8), :] = third_sweep(x0, y0)

    def third_first(x0, y0):
        pr[pl.ds(x0, 8), pl.ds(y0, 8), :] = third_sweep(x0, y0)

    def third_last(x0, y0):
        pr[pl.ds(x0, 8), pl.ds(y0, 8), :] = at(pr, x0, y0) + third_sweep(x0, y0)

    def restart(x0, y0):
        total, centre = stencil(pr, x0, y0)
        weight = at(w, x0, y0)
        b[pl.ds(x0, 8), pl.ds(y0, 8), :] = jnp.where(
            weight > 0.0, weight * (at(r, x0, y0) + total) - centre, 0.0)

    def loop(low, high, body, unroll):
        full = (high - low) // unroll

        def several(i, carry):
            for u in range(unroll):
                body(low + i * unroll + u)
            return carry
        lax.fori_loop(0, full, several, 0)
        for i in range(low + full * unroll, high):
            body(i)

    def region(body, x_low, x_high, y_low, y_high):
        def column(j):
            for i in range(x_low, x_high):
                body(1 + 8 * i, 4 + 8 * j)
        loop(y_low, y_high, column, 1)

    def ring(body, depth, unroll):
        low_y, high_y = depth, nby - 1 - depth
        low_x, high_x = depth, nbx - 1 - depth

        def along_y(j):
            body(1 + 8 * low_x, 4 + 8 * j)
            body(1 + 8 * high_x, 4 + 8 * j)
        loop(low_y, high_y + 1, along_y, unroll)

        def along_x(i):
            body(1 + 8 * i, 4 + 8 * low_y)
            body(1 + 8 * i, 4 + 8 * high_y)
        loop(low_x + 1, high_x, along_x, unroll)

    def interior(body):
        region(body, 1, nbx - 1, 1, nby - 1)

    def inner(body):
        region(body, 2, nbx - 2, 2, nby - 2)

    def frame(body, unroll=4):
        ring(body, 0, unroll)

    def border(body):
        ring(body, 1, 4)

    def gather(turn, x0, y0, side_x, side_y):
        own = at(b, x0, y0, 4)
        before = at(pr, x0, y0, 4)
        row = x0 + lax.broadcasted_iota(jnp.int32, (4, 8, nz), 0)
        column = y0 + lax.broadcasted_iota(jnp.int32, (4, 8, nz), 1)
        total = own
        if side_x is not None:
            total = total + sx[turn, side_x, :, pl.ds(y0 - PADY, 8), :]
        if side_y is not None:
            total = total + sy[turn, side_y, pl.ds(x0 - PADX, 4), :, :]
        cover = 1.0 + (row - PADX < dx_ref[0, pl.ds(y0, 8), :][None]).astype(jnp.float32)
        cover = cover + (x_end - 1 - row < dx_ref[1, pl.ds(y0, 8), :][None]).astype(jnp.float32)
        cover = cover + (column - PADY < dy_ref[0, pl.ds(x0, 4), :, :]).astype(jnp.float32)
        cover = cover + (y_end - 1 - column < dy_ref[1, pl.ds(x0, 4), :, :]).astype(jnp.float32)
        total = total / cover
        if turn == 1:
            total = before + total
        if side_x is None:
            edge = (column < PADY + 4) if side_y == 0 else (column >= y_end - 4)
            total = jnp.where(edge, total, before)
        pr[pl.ds(x0, 4), pl.ds(y0, 8), :] = total

    def gather_all(turn):
        top = x_end - 4
        for side_y, y0 in ((0, PADY), (1, y_end - 8)):
            gather(turn, PADX, y0, 0, side_y)
            gather(turn, top, y0, 1, side_y)

            def along_x(i, carry, y0=y0, side_y=side_y):
                gather(turn, PADX + 4 * i, y0, None, side_y)
                return carry
            lax.fori_loop(1, bx // 4 - 1, along_x, 0)

        def along_y(j, carry):
            gather(turn, PADX, PADY + 8 * j, 0, None)
            gather(turn, top, PADY + 8 * j, 1, None)
            return carry
        lax.fori_loop(1, by // 8 - 1, along_y, 0)

    def returns(turn):
        return [
            remote(b.at[pl.ds(PADX - 4, 4), own_y, :], sx.at[turn, 1], (-1, 0)),
            remote(b.at[pl.ds(x_end, 4), own_y, :], sx.at[turn, 0], (1, 0)),
            remote(b.at[own_x, pl.ds(4, 4), :], sy.at[turn, 1, :, 4:8, :], (0, -1)),
            remote(b.at[own_x, pl.ds(y_end, 4), :], sy.at[turn, 0, :, 0:4, :], (0, 1)),
        ]

    for copy in local:
        copy.wait()
    interior(functools.partial(coefficients, frame=False))
    inner(second_sweep)
    wait_recv(halos)
    frame(functools.partial(coefficients, frame=True), 1)
    frame(second_sweep)
    border(second_sweep)
    frame(third_frame)
    back = returns(0)
    start(back)
    interior(third_first)
    wait_recv(back)
    gather_all(0)
    spread = [halo(pr, PADX, PADY, pr, d, 5) for d in DIRS]
    start(spread)
    interior(restart)
    inner(second_sweep)
    wait_send(back)
    wait_recv(spread)
    frame(restart)
    frame(second_sweep)
    border(second_sweep)
    frame(third_frame)
    back = returns(1)
    start(back)
    wait_send(spread)
    interior(third_last)
    wait_recv(back)
    gather_all(1)
    final = pltpu.make_async_copy(pr.at[own_x, own_y, :], out, lsem.at[0])
    final.start()
    wait_send(halos)
    wait_send(back)
    final.wait()


def shards(n_sub, n_col, perm, accum, rhs, depth_x, depth_y):
    bx, by, nz = perm.shape
    ex, ey = bx + 2 * PADX, by + 2 * PADY
    field = pltpu.VMEM((ex, ey, nz), jnp.float32)
    hbm = pl.BlockSpec(memory_space=pl.ANY)
    vmem = pl.BlockSpec(memory_space=pltpu.VMEM)
    copies = 16 + 4 + 8 + 4
    return pl.pallas_call(
        functools.partial(kernel, n_sub, n_col, bx, by),
        out_shape=jax.ShapeDtypeStruct((bx, by, nz), jnp.float32),
        in_specs=[hbm, hbm, hbm, vmem, vmem],
        out_specs=hbm,
        scratch_shapes=[
            pltpu.VMEM((2, ey, nz), jnp.int32),
            pltpu.VMEM((2, ex, 8, nz), jnp.int32),
            pltpu.VMEM((2, bx, nz), jnp.int32),
        ] + [field] * 9 + [
            pltpu.VMEM((2, 2, 4, by, nz), jnp.float32),
            pltpu.VMEM((2, 2, bx, 8, nz), jnp.float32),
            pltpu.SemaphoreType.DMA((copies,)),
            pltpu.SemaphoreType.DMA((copies,)),
            pltpu.SemaphoreType.DMA((3,)),
        ],
        compiler_params=pltpu.CompilerParams(
            collective_id=0, has_side_effects=True, vmem_limit_bytes=60 * 1024 * 1024),
        cost_estimate=pl.CostEstimate(
            flops=120 * bx * by * nz, bytes_accessed=16 * bx * by * nz, transcendentals=0),
    )(perm, accum, rhs, depth_x, depth_y)


def solution(mesh):
    placed = (
        P("sub", "col", None),
        P("sub", "col", None),
        P("sub", "col", None),
        P("sub", "col"),
        P("sub", "col"),
    )
    return jax.shard_map(
        functools.partial(shards, mesh.shape["sub"], mesh.shape["col"]),
        mesh=mesh, in_specs=placed, out_specs=P("sub", "col", None), check_vma=False
    )
```

```python
import functools

import jax
import jax.numpy as jnp
from jax import lax
from jax.experimental import pallas as pl
from jax.experimental.pallas import tpu as pltpu
from jax.sharding import PartitionSpec as P

OVL = 4
VERTICAL = 0.1
MESH = pl.DeviceIdType.MESH

PADX = 5
PADY = 8
DIRS = ((-1, 0), (1, 0), (0, -1), (0, 1), (-1, -1), (-1, 1), (1, -1), (1, 1))


def recip(value):
    return pl.reciprocal(value, approx=True)


def harmonic(first, second):
    return 2.0 * first * second * recip(first + second)


def kernel(n_sub, n_col, bx, by, perm, accum, rhs, depth_x, depth_y, out,
           dx_ref, dy_ref, lane_y, pm, w, r, b, c, fx, fy, fz, pr, sx, sy, ssem, rsem, lsem):
    nz = 128
    s = lax.axis_index("sub")
    k = lax.axis_index("col")
    ex, ey = bx + 2 * PADX, by + 2 * PADY
    nbx, nby = (bx + 8) // 8, (by + 8) // 8
    x_end, y_end = PADX + bx, PADY + by

    def exists(d):
        ok = None
        for coord, step, count in ((s, d[0], n_sub), (k, d[1], n_col)):
            if step == -1:
                test = coord > 0
            elif step == 1:
                test = coord < count - 1
            else:
                continue
            ok = test if ok is None else ok & test
        return ok

    def device(d):
        return (s + d[0], k + d[1])

    own_x, own_y = pl.ds(PADX, bx), pl.ds(PADY, by)
    local = [
        pltpu.make_async_copy(src, dst.at[own_x, own_y, :], lsem.at[i])
        for i, (src, dst) in enumerate(((perm, pm), (accum, w), (rhs, r)))
    ]
    for copy in local:
        copy.start()

    def fill(ref, value):
        ref[0:PADX, :, :] = jnp.full((PADX, ey, nz), value, jnp.float32)
        ref[x_end:ex, :, :] = jnp.full((PADX, ey, nz), value, jnp.float32)
        ref[PADX:x_end, 0:PADY, :] = jnp.full((bx, PADY, nz), value, jnp.float32)
        ref[PADX:x_end, y_end:ey, :] = jnp.full((bx, PADY, nz), value, jnp.float32)

    fill(pm, 1.0)
    fill(w, 1.0)
    fill(r, 0.0)
    fill(b, 0.0)
    fill(c, 0.0)
    fill(pr, 0.0)
    sx[...] = jnp.zeros(sx.shape, jnp.float32)
    sy[...] = jnp.zeros(sy.shape, jnp.float32)

    dx_ref[...] = jnp.zeros(dx_ref.shape, jnp.int32)
    dy_ref[...] = jnp.zeros(dy_ref.shape, jnp.int32)
    for side in range(2):
        dx_ref[side, own_y, :] = jnp.broadcast_to(depth_x[side:side + 1, :], (nz, by)).T
        lane_y[side] = jnp.broadcast_to(depth_y[:, side:side + 1], (bx, nz))

    def spread_depth(i, carry):
        for side in range(2):
            dy_ref[side, PADX + i] = jnp.broadcast_to(lane_y[side, pl.ds(i, 1), :], (8, nz))
        return carry

    barrier = pltpu.get_barrier_semaphore()
    arrivals = jnp.int32(0)
    for d in DIRS:
        @pl.when(exists(d))
        def _(d=d):
            pl.semaphore_signal(barrier, inc=1, device_id=device(d), device_id_type=MESH)
        arrivals = arrivals + jnp.where(exists(d), 1, 0).astype(jnp.int32)
    pl.semaphore_wait(barrier, arrivals)

    counter = [0]

    def remote(src, dst, d):
        i = counter[0]
        counter[0] += 1
        return d, pltpu.make_async_remote_copy(
            src_ref=src, dst_ref=dst, send_sem=ssem.at[i], recv_sem=rsem.at[i],
            device_id=device(d), device_id_type=MESH)

    def start(copies):
        for d, copy in copies:
            pl.when(exists(d))(copy.start)

    def wait_recv(copies):
        for d, copy in copies:
            pl.when(exists((-d[0], -d[1])))(copy.wait_recv)

    def wait_send(copies):
        for d, copy in copies:
            pl.when(exists(d))(copy.wait_send)

    def halo(src, ox, oy, dst, d, width):
        def span(step, offset, extent, pad, thick):
            if step == 0:
                return pl.ds(offset, extent), pl.ds(pad, extent)
            if step == 1:
                return pl.ds(offset + extent - thick, thick), pl.ds(pad - thick, thick)
            return pl.ds(offset, thick), pl.ds(pad + extent, thick)

        sxs, dxs = span(d[0], ox, bx, PADX, width)
        sys_, dys = span(d[1], oy, by, PADY, width)
        return remote(src.at[sxs, sys_, :], dst.at[dxs, dys, :], d)

    halos = [halo(perm, 0, 0, pm, d, 5) for d in DIRS]
    halos += [halo(accum, 0, 0, w, d, 4) for d in DIRS[:4]]
    halos += [halo(rhs, 0, 0, r, d, 4) for d in DIRS[:4]]
    start(halos)
    lax.fori_loop(0, bx, spread_depth, 0, unroll=8)

    def at(ref, x0, y0, rows=8, columns=8):
        return ref[pl.ds(x0, rows), pl.ds(y0, columns), :]

    def stencil(ref, x0, y0):
        wide = at(ref, x0 - 1, y0, 10)
        centre = wide[1:9]
        face = at(fx, x0 - 1, y0, 9)
        total = face[0:8] * wide[0:8] + face[1:9] * wide[2:10]
        total = total + at(fy, x0, y0) * at(ref, x0, y0 - 1)
        total = total + at(fy, x0, y0 + 1) * at(ref, x0, y0 + 1)
        up = at(fz, x0, y0)
        total = total + up * pltpu.roll(centre, nz - 1, 2)
        total = total + pltpu.roll(up * centre, 1, 2)
        return total, centre

    def coefficients(x0, y0, frame):
        wide = at(pm, x0 - 1, y0, 10)
        centre = wide[1:9]
        across_x = harmonic(wide[0:9], wide[1:10])
        across_y0 = harmonic(at(pm, x0, y0 - 1), centre)
        across_y1 = harmonic(centre, at(pm, x0, y0 + 1))
        lane = lax.broadcasted_iota(jnp.int32, (8, 8, nz), 2)
        up = VERTICAL * harmonic(centre, pltpu.roll(centre, nz - 1, 2))
        up = jnp.where(lane < nz - 1, up, 0.0)
        if frame:
            row = x0 - 1 + lax.broadcasted_iota(jnp.int32, (9, 8, nz), 0)
            shut = (row == jnp.where(s == 0, PADX - 1, -1)) | (
                row == jnp.where(s == n_sub - 1, x_end - 1, -1))
            across_x = jnp.where(shut, 0.0, across_x)
            column = y0 + lax.broadcasted_iota(jnp.int32, (8, 8, nz), 1)
            first = jnp.where(k == 0, PADY, -1)
            last = jnp.where(k == n_col - 1, y_end, -1)
            across_y0 = jnp.where((column == first) | (column == last), 0.0, across_y0)
            across_y1 = jnp.where((column + 1 == first) | (column + 1 == last), 0.0, across_y1)
        faces = (across_x[0:8] + across_x[1:9] + across_y0 + across_y1
                 + up + pltpu.roll(up, 1, 2))
        if frame:
            row = row[0:8] + 1
            low_x, high_x = dx_ref[0, pl.ds(y0, 8), :], dx_ref[1, pl.ds(y0, 8), :]
            low_y, high_y = dy_ref[0, pl.ds(x0, 8), :, :], dy_ref[1, pl.ds(x0, 8), :, :]
            member = (row >= PADX) & (row < x_end) & (column >= PADY) & (column < y_end)
            member = member | ((row < PADX) & (PADX - 1 - row < low_x[None]))
            member = member | ((row >= x_end) & (row - x_end < high_x[None]))
            member = member | ((column < PADY) & (PADY - 1 - column < low_y))
            member = member | ((column >= y_end) & (column - y_end < high_y))
            c[pl.ds(x0, 8), pl.ds(y0, 8), :] = jnp.where(member, faces, -1.0)
        fx[pl.ds(x0 - 1, 9), pl.ds(y0, 8), :] = across_x
        fy[pl.ds(x0, 8), pl.ds(y0, 8), :] = across_y0
        fy[pl.ds(x0, 8), pl.ds(y0 + 1, 8), :] = across_y1
        fz[pl.ds(x0, 8), pl.ds(y0, 8), :] = up
        if not frame:
            inverse = recip(at(w, x0, y0) + faces)
            w[pl.ds(x0, 8), pl.ds(y0, 8), :] = inverse
            b[pl.ds(x0, 8), pl.ds(y0, 8), :] = inverse * at(r, x0, y0)

    def weights(x0, y0):
        faces = at(c, x0, y0)
        inverse = jnp.where(faces >= 0.0, recip(at(w, x0, y0) + jnp.maximum(faces, 0.0)), 0.0)
        w[pl.ds(x0, 8), pl.ds(y0, 8), :] = inverse
        b[pl.ds(x0, 8), pl.ds(y0, 8), :] = inverse * at(r, x0, y0)

    def second_sweep(x0, y0):
        total, _ = stencil(b, x0, y0)
        c[pl.ds(x0, 8), pl.ds(y0, 8), :] = at(b, x0, y0) + at(w, x0, y0) * total

    def third_sweep(x0, y0):
        total, _ = stencil(c, x0, y0)
        return at(b, x0, y0) + at(w, x0, y0) * total

    def third_frame(x0, y0):
        b[pl.ds(x0, 8), pl.ds(y0, 8), :] = third_sweep(x0, y0)

    def third_first(x0, y0):
        pr[pl.ds(x0, 8), pl.ds(y0, 8), :] = third_sweep(x0, y0)

    def third_last(x0, y0):
        pr[pl.ds(x0, 8), pl.ds(y0, 8), :] = at(pr, x0, y0) + third_sweep(x0, y0)

    def restart(x0, y0):
        total, centre = stencil(pr, x0, y0)
        weight = at(w, x0, y0)
        b[pl.ds(x0, 8), pl.ds(y0, 8), :] = jnp.where(
            weight > 0.0, weight * (at(r, x0, y0) + total) - centre, 0.0)

    def loop(low, high, body, unroll):
        full = (high - low) // unroll

        def several(i, carry):
            for u in range(unroll):
                body(low + i * unroll + u)
            return carry
        lax.fori_loop(0, full, several, 0)
        for i in range(low + full * unroll, high):
            body(i)

    def region(body, x_low, x_high, y_low, y_high):
        def column(j):
            for i in range(x_low, x_high):
                body(1 + 8 * i, 4 + 8 * j)
        loop(y_low, y_high, column, 2)

    def ring(body, depth, unroll, between=lambda: None):
        low_y, high_y = depth, nby - 1 - depth
        low_x, high_x = depth, nbx - 1 - depth

        def along_y(j):
            body(1 + 8 * low_x, 4 + 8 * j)
            body(1 + 8 * high_x, 4 + 8 * j)
        loop(low_y, high_y + 1, along_y, unroll)
        between()

        def along_x(i):
            body(1 + 8 * i, 4 + 8 * low_y)
            body(1 + 8 * i, 4 + 8 * high_y)
        loop(low_x + 1, high_x, along_x, unroll)

    def interior(body):
        region(body, 1, nbx - 1, 1, nby - 1)

    def inner(body):
        region(body, 2, nbx - 2, 2, nby - 2)

    def frame(body, unroll=4, between=lambda: None):
        ring(body, 0, unroll, between)

    def border(body):
        ring(body, 1, 4)

    def gather(turn, x0, y0, side_x, side_y):
        own = at(b, x0, y0, 4)
        before = at(pr, x0, y0, 4)
        row = x0 + lax.broadcasted_iota(jnp.int32, (4, 8, nz), 0)
        column = y0 + lax.broadcasted_iota(jnp.int32, (4, 8, nz), 1)
        total = own
        if side_x is not None:
            total = total + sx[turn, side_x, :, pl.ds(y0 - PADY, 8), :]
        if side_y is not None:
            total = total + sy[turn, side_y, pl.ds(x0 - PADX, 4), :, :]
        cover = 1.0 + (row - PADX < dx_ref[0, pl.ds(y0, 8), :][None]).astype(jnp.float32)
        cover = cover + (x_end - 1 - row < dx_ref[1, pl.ds(y0, 8), :][None]).astype(jnp.float32)
        cover = cover + (column - PADY < dy_ref[0, pl.ds(x0, 4), :, :]).astype(jnp.float32)
        cover = cover + (y_end - 1 - column < dy_ref[1, pl.ds(x0, 4), :, :]).astype(jnp.float32)
        total = total / cover
        if turn == 1:
            total = before + total
        if side_x is None:
            edge = (column < PADY + 4) if side_y == 0 else (column >= y_end - 4)
            total = jnp.where(edge, total, before)
        pr[pl.ds(x0, 4), pl.ds(y0, 8), :] = total

    def gather_all(turn):
        top = x_end - 4
        for side_y, y0 in ((0, PADY), (1, y_end - 8)):
            gather(turn, PADX, y0, 0, side_y)
            gather(turn, top, y0, 1, side_y)

            def along_x(i, carry, y0=y0, side_y=side_y):
                gather(turn, PADX + 4 * i, y0, None, side_y)
                return carry
            lax.fori_loop(1, bx // 4 - 1, along_x, 0)

        def along_y(j, carry):
            gather(turn, PADX, PADY + 8 * j, 0, None)
            gather(turn, top, PADY + 8 * j, 1, None)
            return carry
        lax.fori_loop(1, by // 8 - 1, along_y, 0)

    def returns(turn):
        return [
            remote(b.at[pl.ds(PADX - 4, 4), own_y, :], sx.at[turn, 1], (-1, 0)),
            remote(b.at[pl.ds(x_end, 4), own_y, :], sx.at[turn, 0], (1, 0)),
            remote(b.at[own_x, pl.ds(4, 4), :], sy.at[turn, 1, :, 4:8, :], (0, -1)),
            remote(b.at[own_x, pl.ds(y_end, 4), :], sy.at[turn, 0, :, 0:4, :], (0, 1)),
        ]

    for copy in local:
        copy.wait()
    interior(functools.partial(coefficients, frame=False))
    wait_recv(halos[:8])
    frame(functools.partial(coefficients, frame=True), 1)
    inner(second_sweep)
    wait_recv(halos[8:])
    frame(weights)
    frame(second_sweep)
    border(second_sweep)
    back = returns(0)
    frame(third_frame, 4, lambda: start(back[:2]))
    start(back[2:])
    interior(third_first)
    wait_recv(back)
    gather_all(0)
    spread = [halo(pr, PADX, PADY, pr, d, 5) for d in DIRS]
    start(spread)
    interior(restart)
    inner(second_sweep)
    wait_send(back)
    wait_recv(spread)
    frame(restart)
    frame(second_sweep)
    border(second_sweep)
    back = returns(1)
    frame(third_frame, 4, lambda: start(back[:2]))
    start(back[2:])
    wait_send(spread)
    interior(third_last)

    def store(i, x0, rows, y0, columns):
        return pltpu.make_async_copy(
            pr.at[pl.ds(PADX + x0, rows), pl.ds(PADY + y0, columns), :],
            out.at[pl.ds(x0, rows), pl.ds(y0, columns), :], lsem.at[i])

    middle = store(0, 4, bx - 8, 8, by - 16)
    edges = [store(1, 0, 4, 0, by), store(2, bx - 4, 4, 0, by),
             store(3, 4, bx - 8, 0, 8), store(4, 4, bx - 8, by - 8, 8)]
    middle.start()
    wait_recv(back)
    gather_all(1)
    for copy in edges:
        copy.start()
    wait_send(halos)
    wait_send(back)
    for copy in (*edges, middle):
        copy.wait()


def relay(source, target, held, sem):
    rows = source.shape[0] // 8
    spans = [pl.ds(i * rows, rows) for i in range(8)]
    reads = [pltpu.make_async_copy(source.at[span], held.at[span], sem.at[0, i])
             for i, span in enumerate(spans)]
    writes = [pltpu.make_async_copy(held.at[span], target.at[span], sem.at[1, i])
              for i, span in enumerate(spans)]
    for copy in reads:
        copy.start()
    for read, write in zip(reads, writes):
        read.wait()
        write.start()
    for copy in writes:
        copy.wait()


def shards(n_sub, n_col, perm, accum, rhs, depth_x, depth_y):
    bx, by, nz = perm.shape
    ex, ey = bx + 2 * PADX, by + 2 * PADY
    field = pltpu.VMEM((ex, ey, nz), jnp.float32)
    hbm = pl.BlockSpec(memory_space=pl.ANY)
    vmem = pl.BlockSpec(memory_space=pltpu.VMEM)
    copies = 16 + 4 + 8 + 4
    result = pl.pallas_call(
        functools.partial(kernel, n_sub, n_col, bx, by),
        out_shape=jax.ShapeDtypeStruct((bx, by, nz), jnp.float32),
        in_specs=[hbm, hbm, hbm, vmem, vmem],
        out_specs=hbm,
        scratch_shapes=[
            pltpu.VMEM((2, ey, nz), jnp.int32),
            pltpu.VMEM((2, ex, 8, nz), jnp.int32),
            pltpu.VMEM((2, bx, nz), jnp.int32),
        ] + [field] * 9 + [
            pltpu.VMEM((2, 2, 4, by, nz), jnp.float32),
            pltpu.VMEM((2, 2, bx, 8, nz), jnp.float32),
            pltpu.SemaphoreType.DMA((copies,)),
            pltpu.SemaphoreType.DMA((copies,)),
            pltpu.SemaphoreType.DMA((5,)),
        ],
        compiler_params=pltpu.CompilerParams(
            collective_id=0, has_side_effects=True, vmem_limit_bytes=60 * 1024 * 1024),
        cost_estimate=pl.CostEstimate(
            flops=120 * bx * by * nz, bytes_accessed=16 * bx * by * nz, transcendentals=0),
    )(perm, accum, rhs, depth_x, depth_y)
    return pl.pallas_call(
        relay,
        out_shape=jax.ShapeDtypeStruct((bx, by, nz), jnp.float32),
        in_specs=[hbm], out_specs=hbm,
        scratch_shapes=[pltpu.VMEM((bx, by, nz), jnp.float32), pltpu.SemaphoreType.DMA((2, 8))],
        compiler_params=pltpu.CompilerParams(vmem_limit_bytes=16 * 1024 * 1024),
    )(result)


def solution(mesh):
    placed = (
        P("sub", "col", None),
        P("sub", "col", None),
        P("sub", "col", None),
        P("sub", "col"),
        P("sub", "col"),
    )
    return jax.shard_map(
        functools.partial(shards, mesh.shape["sub"], mesh.shape["col"]),
        mesh=mesh, in_specs=placed, out_specs=P("sub", "col", None), check_vma=False
    )
```
